512 devices in a mesh: ctx: 64 (over y_hi, z, core), head: 8 (over y_lo, x).
Axes of the slice: x: 4, y: 8 (y_hi: 4, y_lo: 2; y = y_hi * 2 + y_lo), z: 8, core: 2. Of those that a mesh axis runs over, the one named last changes fastest.
Arguments:
- queries: bfloat16 [256, 16384], P('ctx', 'head'), may hold values from -7 to 7
- grad_out: bfloat16 [256, 16384], P('ctx', 'head'), may hold values from -384 to 384
- outputs: bfloat16 [256, 16384], P('ctx', 'head'), may hold values from -6 to 6
- lse_self: float32 [256, 128], P('ctx', 'head'), may hold values from 0 to 20
- prompt_keys: bfloat16 [16384, 1024], P(('ctx', 'head')), may hold values from -11 to 11
- prompt_values: bfloat16 [16384, 1024], P(('ctx', 'head')), may hold values from -6 to 6
- resp_len: int32 [4], replicated, may hold values from 16 to 64, as said below
- prompt_end: int32 [4], replicated, may hold values from 8192 to 16384, as said below
Outputs:
- query_grad: bfloat16 [256, 16384], P('ctx', 'head')
- prompt_key_grad: bfloat16 [16384, 1024], P(('ctx', 'head'))
- prompt_value_grad: bfloat16 [16384, 1024], P(('ctx', 'head'))
The draws below stay inside these ranges and needn't reach their ends.
Inputs may be any that keep to these rules, and one draw needn't show every extreme that they name: `resp_len`: at least one response has all 64 rows live. `prompt_end`: at least one response sees the whole prompt.
All inputs are finite; a program needn't handle non-finite values.
Results may differ from the reference program's by a relative error of at most 0.013.
Values may be sent and summed in bfloat16 or wider, within the bound.
A program may use at most 64 MiB of HBM per device.

```python
import math
import jax
import jax.numpy as jnp
from jax import lax

QH = 128
KVH = 8
DH = 128
RESP_LEN = 64
PROMPT = 16384
ROWS = 256
NRESP = 4


def draw_queries(key, part):
    key = jax.random.fold_in(key, 5)
    key_base, key_rows = jax.random.split(key)
    base = jax.random.truncated_normal(key_base, -4.0, 4.0, (ROWS, QH * DH), jnp.float32)
    row_scale = jnp.exp(jax.random.uniform(key_rows, (ROWS, 1), jnp.float32, -0.5, 0.5))
    values = base * row_scale
    return values.astype(jnp.bfloat16)


def draw_prompt_keys(key, part):
    key = jax.random.fold_in(key, 7)
    key_base, key_rows = jax.random.split(key)
    position = jnp.arange(PROMPT, dtype=jnp.float32)[:, None] / PROMPT
    rough = jnp.exp(jax.random.uniform(key_rows, (PROMPT, 1), jnp.float32, -0.6, 0.6))
    base = jax.random.truncated_normal(key_base, -4.0, 4.0, (PROMPT, KVH * DH), jnp.float32)
    values = base * (0.5 + position) * rough
    return values.astype(jnp.bfloat16)


def draw_lse_self(key, part):
    key = jax.random.fold_in(key, 9)
    offset = jax.random.uniform(key, (ROWS, QH), jnp.float32, -1.0, 2.5)
    return (math.log(PROMPT) + offset).astype(jnp.float32)


def draw_resp_len(key, part):
    key = jax.random.fold_in(key, 13)
    key_vals, key_full = jax.random.split(key)
    values = jax.random.randint(key_vals, (NRESP,), RESP_LEN // 4, RESP_LEN + 1, jnp.int32)
    chosen = jax.random.randint(key_full, (), 0, NRESP, jnp.int32)
    return jnp.where(jnp.arange(NRESP, dtype=jnp.int32) == chosen, RESP_LEN, values).astype(jnp.int32)


def draw_prompt_end(key, part):
    key = jax.random.fold_in(key, 17)
    key_vals, key_full = jax.random.split(key)
    values = jax.random.randint(key_vals, (NRESP,), PROMPT // 2, PROMPT + 1, jnp.int32)
    chosen = jax.random.randint(key_full, (), 0, NRESP, jnp.int32)
    return jnp.where(jnp.arange(NRESP, dtype=jnp.int32) == chosen, PROMPT, values).astype(jnp.int32)


def levels(own_key, extent, pieces, smallest, largest):
    factor_of = 1.0
    for dim, blocks in pieces:
        heights = jax.random.uniform(jax.random.fold_in(jax.random.fold_in(own_key, 6), dim), (blocks,), jnp.float32, smallest / len(pieces), largest / len(pieces))
        factor_of = factor_of * jnp.repeat(jnp.exp(heights), extent[dim] // blocks).reshape((-1,) + (1,) * (len(extent) - 1 - dim))
    return factor_of


def gaussian(stream_key, dims, width, limit, cuts=(), kind=jnp.bfloat16):
    values = jax.random.normal(stream_key, dims, jnp.float32) * width
    if len(cuts) > 0:
        values = levels(stream_key, dims, cuts, -0.22, 0.18) * values
    return jnp.clip(values, min=-limit, max=limit).astype(kind)


def setup_inputs(seed: int = 0) -> dict:
    key_list = jax.random.split(jax.random.key(seed), 9)
    return {
        "queries": draw_queries(jax.random.fold_in(key_list[8], 71), 0),
        "grad_out": gaussian(key_list[1], (ROWS, QH * DH), 64.0, 384.0, ((0, 64), (1, 8))),
        "outputs": gaussian(key_list[2], (ROWS, QH * DH), 1.0, 6.0, ((0, 64), (1, 8))),
        "lse_self": draw_lse_self(jax.random.fold_in(key_list[8], 71), 0),
        "prompt_keys": draw_prompt_keys(jax.random.fold_in(key_list[8], 71), 0),
        "prompt_values": gaussian(key_list[5], (PROMPT, KVH * DH), 1.0, 6.0, ((0, 512),)),
        "resp_len": draw_resp_len(jax.random.fold_in(key_list[8], 71), 0),
        "prompt_end": draw_prompt_end(jax.random.fold_in(key_list[8], 71), 0),
    }


MASKED_SCORE = -1.0e30


def head_terms(query_head, grad_head, output_head, self_lse, key_group, value_group, visible, live_rows):
    score_scale = DH ** -0.5
    scores = jnp.dot(query_head, key_group.T, preferred_element_type=jnp.float32) * score_scale
    scores = jnp.where(visible, scores, MASKED_SCORE)
    row_peak = jnp.max(scores, axis=1)
    prompt_lse = row_peak + jnp.log(jnp.sum(jnp.where(visible, jnp.exp(scores - row_peak[:, None]), 0.0), axis=1))
    higher = jnp.maximum(prompt_lse, self_lse)
    full_lse = higher + jnp.log(jnp.exp(prompt_lse - higher) + jnp.exp(self_lse - higher))
    prob = jnp.where(visible, jnp.exp(scores - full_lse[:, None]), 0.0) * live_rows[:, None]
    row_dots = jnp.sum(grad_head.astype(jnp.float32) * output_head.astype(jnp.float32), axis=1)
    dprob = jnp.dot(grad_head, value_group.T, preferred_element_type=jnp.float32)
    dscore = (prob * (dprob - row_dots[:, None])).astype(jnp.bfloat16)
    value_grad = jnp.dot(prob.astype(jnp.bfloat16).T, grad_head, preferred_element_type=jnp.float32)
    key_grad = jnp.dot(dscore.T, query_head, preferred_element_type=jnp.float32) * score_scale
    query_grad = jnp.dot(dscore, key_group, preferred_element_type=jnp.float32) * score_scale
    return query_grad, key_grad, value_grad


def reference(queries, grad_out, outputs, lse_self, prompt_keys, prompt_values, resp_len, prompt_end):
    row_count = queries.shape[0]
    prompt_len = prompt_keys.shape[0]
    per_group = QH // KVH
    row_ids = jnp.arange(row_count, dtype=jnp.int32)
    resp_index = row_ids // RESP_LEN
    live_rows = ((row_ids % RESP_LEN) < resp_len[resp_index]).astype(jnp.float32)
    visible = jnp.arange(prompt_len, dtype=jnp.int32)[None, :] < prompt_end[resp_index][:, None]

    def group_step(unused, group_index):
        key_group = lax.dynamic_slice_in_dim(prompt_keys, group_index * DH, DH, 1)
        value_group = lax.dynamic_slice_in_dim(prompt_values, group_index * DH, DH, 1)

        def head_step(totals, head_index):
            head_number = group_index * per_group + head_index
            query_head = lax.dynamic_slice_in_dim(queries, head_number * DH, DH, 1)
            grad_head = lax.dynamic_slice_in_dim(grad_out, head_number * DH, DH, 1)
            output_head = lax.dynamic_slice_in_dim(outputs, head_number * DH, DH, 1)
            self_lse = lax.dynamic_index_in_dim(lse_self, head_number, 1, keepdims=False)
            query_grad, key_grad, value_grad = head_terms(query_head, grad_head, output_head, self_lse, key_group, value_group, visible, live_rows)
            return (totals[0] + key_grad, totals[1] + value_grad), query_grad

        zero_sums = (jnp.zeros((prompt_len, DH), jnp.float32), jnp.zeros((prompt_len, DH), jnp.float32))
        (key_sum, value_sum), query_grads = lax.scan(head_step, zero_sums, jnp.arange(per_group, dtype=jnp.int32))
        return unused, (query_grads, key_sum, value_sum)

    _, (query_grads, key_sums, value_sums) = lax.scan(group_step, jnp.zeros((), jnp.float32), jnp.arange(KVH, dtype=jnp.int32))
    query_grad = jnp.transpose(query_grads, (2, 0, 1, 3)).reshape(row_count, QH * DH).astype(jnp.bfloat16)
    key_grad = jnp.transpose(key_sums, (1, 0, 2)).reshape(prompt_len, KVH * DH).astype(jnp.bfloat16)
    value_grad = jnp.transpose(value_sums, (1, 0, 2)).reshape(prompt_len, KVH * DH).astype(jnp.bfloat16)
    return (query_grad, key_grad, value_grad)
```

```python
import functools

import jax
import jax.numpy as jnp
from jax import lax
from jax.experimental import pallas as pl
from jax.experimental.pallas import tpu as pltpu
from jax.sharding import PartitionSpec as P

MESH = pl.DeviceIdType.MESH
F32 = jnp.float32
BF16 = jnp.bfloat16

DH = 128
HEADS = 8
PER_GROUP = 16
OWN_ROWS = 4
RESP_LEN = 64
YS, ZS = 4, 8
OWN_Q = OWN_ROWS * PER_GROUP
SLOTS = 2 * ZS
CHUNK = 2 * OWN_Q
NQ = SLOTS * OWN_Q
PIECE = 32
PIECES = 16
NT = 2 * PIECES * PIECE
SCALE = DH**-0.5
MASKED = -1e30
FLOOR = -1e20
DEAD = 1e30

NT_DIMS = (((1,), (1,)), ((), ()))


def kernel(
    q_in, do_in, o_in, lse_in, k_in, v_in, len_in, end_in,
    dq_out, dk_out, dv_out,
    qbuf, dobuf, kvs, kvbuf, lsebuf, mrow, lrow, posbuf, kt, ebuf, dsbuf, wq, wdo,
    dqs, dqr, fbuf, sib_s, sib_r, dkvs, dkvr,
    q_ss, q_rs, do_ss, do_rs, kv_ss, kv_rs, fwd_ss, fwd_rs, st_ss, st_rs, dq_ss, dq_rs,
    sib_ss, sib_rs, out_ss, out_rs,
):
    ctx = lax.axis_index("ctx")
    head = lax.axis_index("head")
    core = lax.rem(ctx, 2)
    z = lax.rem(ctx // 2, ZS)
    y = ctx // (2 * ZS)

    def device(yy, zz, cc, hh):
        return {
            "ctx": (lax.rem(yy + YS, YS) * ZS + lax.rem(zz + ZS, ZS)) * 2 + cc,
            "head": lax.rem(hh + HEADS, HEADS),
        }

    low = head < 4
    row_slots = [(s % 2 * 2, s // 2) for s in range(SLOTS)]

    def back_slot(dy, dz):
        return ((ZS - dz) % ZS) * 2 + dy // 2

    def row_device(s):
        dy, dz = row_slots[s]
        return device(y + dy, z + dz, core, head)

    def source_head(d):
        return lax.rem(head + HEADS - d, HEADS)

    def piece_y(p):
        if p < HEADS:
            return y
        return y + jnp.where(source_head(p - HEADS) < 4, 1, -1)

    def piece_device(p):
        return device(piece_y(p), z, core, source_head(p % HEADS))

    def user_device(p):
        if p < HEADS:
            return device(y, z, core, head + p)
        return device(y + jnp.where(low, -1, 1), z, core, head + p - HEADS)

    sibling = device(y, z, 1 - core, head)

    barrier = pltpu.get_barrier_semaphore()
    greeted = [row_device(s) for s in range(1, SLOTS)]
    greeted += [user_device(p) for p in range(1, PIECES)]
    greeted += [
        device(y + jnp.where(low, 1, -1), z, core, jnp.where(low, 0, 4) + i) for i in range(4)
    ]
    greeted += [sibling]
    for target in greeted:
        pl.semaphore_signal(barrier, inc=1, device_id=target, device_id_type=MESH)

    qbuf[0] = q_in[...]
    dobuf[0, :OWN_Q] = do_in[...]
    prod = do_in[...].astype(F32) * o_in[...].astype(F32)
    dots = jnp.sum(prod.T, axis=0, keepdims=True)
    dots = jnp.concatenate([dots, jnp.zeros((1, DH - OWN_Q), F32)], axis=1)
    high = dots.astype(BF16).astype(F32)
    middle = (dots - high).astype(BF16).astype(F32)
    rest = dots - high - middle
    dobuf[0, OWN_Q:] = jnp.concatenate(
        [high, middle, rest, jnp.zeros((13, DH), F32)], axis=0
    ).astype(BF16)
    for g in range(HEADS):
        kvs[g, 0] = k_in[:, g * DH : (g + 1) * DH]
        kvs[g, 1] = v_in[:, g * DH : (g + 1) * DH]
    pl.semaphore_wait(barrier, len(greeted))

    def copy(src, dst, ss, rs, i, target):
        return pltpu.make_async_remote_copy(
            src_ref=src, dst_ref=dst, send_sem=ss.at[i], recv_sem=rs.at[i],
            device_id=target, device_id_type=MESH,
        )

    sent = []

    def send(src, dst, ss, rs, i, target):
        started = copy(src, dst, ss, rs, i, target)
        started.start()
        sent.append(started)

    def kv_copy(p):
        return (
            kvs.at[lax.rem(head + p % HEADS, HEADS)], kvbuf.at[0, :, p], kv_ss, kv_rs, p,
            user_device(p),
        )

    for p in range(1, PIECES):
        send(*kv_copy(p))
    for s in range(1, SLOTS):
        t = back_slot(*row_slots[s])
        send(qbuf.at[0], qbuf.at[t], q_ss, q_rs, t, row_device(s))
    for s in range(1, SLOTS):
        t = back_slot(*row_slots[s])
        send(dobuf.at[0], dobuf.at[t], do_ss, do_rs, t, row_device(s))

    kvbuf[0, :, 0] = kvs[head]

    iota = lax.broadcasted_iota(jnp.int32, (PIECE, DH), 0)
    for part in range(2):
        part_core = core if part == 0 else 1 - core
        for p in range(PIECES):
            place = (lax.rem(piece_y(p) + YS, YS) * ZS + z) * 2 + part_core
            base = place * (HEADS * PIECE) + source_head(p % HEADS) * PIECE
            posbuf[pl.ds((part * PIECES + p) * PIECE, PIECE), :] = iota + base
    lane = lax.broadcasted_iota(jnp.int32, (1, DH), 1)
    limit = jnp.where(lane < OWN_Q, end_in[y], end_in[lax.rem(y + 2, YS)])

    lane64 = lax.broadcasted_iota(jnp.int32, (OWN_ROWS, OWN_Q), 1)
    sub64 = lax.broadcasted_iota(jnp.int32, (OWN_ROWS, OWN_Q), 0)
    spread = jnp.zeros((OWN_ROWS, OWN_Q), F32)
    for h in range(PER_GROUP):
        spread = jnp.where(lane64 // OWN_ROWS == h, lse_in[:, h : h + 1], spread)
    own_lse = jnp.sum(
        jnp.where(lane64 % OWN_ROWS == sub64, spread, 0.0), axis=0, keepdims=True
    )
    own_lse = jnp.concatenate([own_lse, jnp.full((1, DH - OWN_Q), MASKED, F32)], axis=1)
    row_in_resp = z * (2 * OWN_ROWS) + core * OWN_ROWS + lane % OWN_ROWS
    dead = jnp.logical_and(lane < OWN_Q, row_in_resp >= len_in[y])

    for p in range(1, PIECES):
        copy(*kv_copy(p)).wait_recv()
    for i in range(2):
        send(kvbuf.at[0, i], kvbuf.at[1, i], fwd_ss, fwd_rs, i, sibling)
    for i in range(2):
        copy(kvbuf.at[0, i], kvbuf.at[1, i], fwd_ss, fwd_rs, i, sibling).wait_recv()
    for s in range(1, SLOTS):
        copy(qbuf.at[0], qbuf.at[s], q_ss, q_rs, s, sibling).wait_recv()

    keys = kvbuf[:, 0].reshape(NT, DH)
    kt[...] = keys.T

    def score_step(c, carry):
        queries = qbuf[pl.ds(2 * c, 2)].reshape(CHUNK, DH)
        scores = lax.dot_general(
            kvbuf[:, 0].reshape(NT, DH), queries, NT_DIMS, preferred_element_type=F32
        ) * SCALE
        scores = jnp.where(posbuf[...] < limit, scores, MASKED)
        peak = jnp.maximum(jnp.max(scores, axis=0, keepdims=True), FLOOR)
        terms = jnp.exp(scores - peak)
        total = jnp.sum(terms, axis=0, keepdims=True)
        ebuf[:, pl.ds(pl.multiple_of(c * CHUNK, CHUNK), CHUNK)] = terms.astype(BF16)
        mrow[pl.ds(c, 1), :] = peak
        lrow[pl.ds(c, 1), :] = total
        return carry

    lax.fori_loop(0, SLOTS // 2, score_step, 0)

    peaks = mrow[...]
    totals = lrow[...]
    local_lse = jnp.where(totals > 0.0, peaks + jnp.log(jnp.maximum(totals, 1e-37)), MASKED)
    first = local_lse[0:1]
    higher = jnp.maximum(first, own_lse)
    joined = higher + jnp.log(jnp.exp(first - higher) + jnp.exp(own_lse - higher))
    joined = jnp.where(lane < OWN_Q, jnp.where(dead, DEAD, joined), first)
    lsebuf[0] = jnp.concatenate([joined, local_lse[1:]], axis=0)
    for s in range(1, SLOTS):
        t = back_slot(*row_slots[s])
        send(lsebuf.at[0], lsebuf.at[t], st_ss, st_rs, t, row_device(s))
    lrow[...] = jnp.where(totals > 0.0, SCALE / jnp.maximum(totals, 1e-37), 0.0)

    for s in range(1, SLOTS):
        copy(dobuf.at[0], dobuf.at[s], do_ss, do_rs, s, sibling).wait_recv()

    def dscore_step(c, carry):
        pair = dobuf[pl.ds(2 * c, 2)]
        grads = pair[:, :OWN_Q].reshape(CHUNK, DH)
        parts = pair[:, OWN_Q:].astype(F32)
        dots_pair = parts[:, 0:1] + parts[:, 1:2] + parts[:, 2:3]
        dots_row = jnp.concatenate([dots_pair[0, :, :OWN_Q], dots_pair[1, :, :OWN_Q]], axis=1)
        dprob = lax.dot_general(
            kvbuf[:, 1].reshape(NT, DH), grads, NT_DIMS, preferred_element_type=F32
        )
        columns = pl.ds(pl.multiple_of(c * CHUNK, CHUNK), CHUNK)
        dscore = (ebuf[:, columns].astype(F32) * (dprob - dots_row)).astype(BF16)
        dsbuf[:, columns] = dscore
        dq_t = jnp.dot(kt[...], dscore, preferred_element_type=F32)
        dq_t = dq_t * lrow[pl.ds(c, 1), :]
        dqs[pl.ds(2 * c, 2)] = dq_t.T.astype(BF16).reshape(2, OWN_Q, DH)
        return carry

    lax.fori_loop(0, SLOTS // 2, dscore_step, 0)

    for s in range(1, SLOTS):
        t = back_slot(*row_slots[s])
        send(dqs.at[s], dqr.at[t], dq_ss, dq_rs, t, row_device(s))

    aligned = []
    for s in range(SLOTS):
        if s > 0:
            copy(lsebuf.at[0], lsebuf.at[s], st_ss, st_rs, s, sibling).wait_recv()
        part = lsebuf[s]
        dy, dz = row_slots[s]
        if dz:
            part = jnp.concatenate([part[ZS - dz :], part[: ZS - dz]], axis=0)
        if dy:
            part = jnp.concatenate([part[:, OWN_Q:], part[:, :OWN_Q]], axis=1)
        aligned.append(part)
    top = functools.reduce(jnp.maximum, aligned)
    total = functools.reduce(jnp.add, [jnp.exp(part - top) for part in aligned])
    full_lse = top + jnp.log(total)
    for s in range(SLOTS):
        mine = local_lse[0:1] if s == 0 else aligned[s][0:1]
        fbuf[s : s + 1, :] = jnp.exp(mine - full_lse[0:1])
    weight = jnp.exp(peaks - full_lse).T
    for c in range(SLOTS // 2):
        rows = slice(c * CHUNK, (c + 1) * CHUNK)
        column = weight[:, c : c + 1]
        wq[rows] = (
            qbuf[2 * c : 2 * c + 2].reshape(CHUNK, DH).astype(F32) * (column * SCALE)
        ).astype(BF16)
        wdo[rows] = (
            dobuf[2 * c : 2 * c + 2, :OWN_Q].reshape(CHUNK, DH).astype(F32) * column
        ).astype(BF16)

    half = PIECES * PIECE
    block = 256
    for i, (probs, weighted) in enumerate(((dsbuf, wq), (ebuf, wdo))):
        for b in range(half // block):
            rows = slice(half + b * block, half + (b + 1) * block)
            part = jnp.dot(probs[rows], weighted[...], preferred_element_type=F32)
            per = block // PIECE
            sib_s[i, b * per : (b + 1) * per] = part.astype(BF16).reshape(per, PIECE, DH)
        send(sib_s.at[i], sib_r.at[i], sib_ss, sib_rs, i, sibling)
    for i, (probs, weighted) in enumerate(((dsbuf, wq), (ebuf, wdo))):
        copy(sib_s.at[i], sib_r.at[i], sib_ss, sib_rs, i, sibling).wait_recv()
        for b in range(half // block):
            rows = slice(b * block, (b + 1) * block)
            part = jnp.dot(probs[rows], weighted[...], preferred_element_type=F32)
            per = block // PIECE
            pieces = slice(b * per, (b + 1) * per)
            dkvs[i, pieces] = (
                part.reshape(per, PIECE, DH) + sib_r[i, pieces].astype(F32)
            ).astype(BF16)

    for p in range(1, PIECES):
        send(dkvs.at[:, p], dkvr.at[p], out_ss, out_rs, p, piece_device(p))
    dkvr[0] = dkvs[:, 0]

    shares = fbuf[...].T
    grad = dqs[0].astype(F32) * shares[:OWN_Q, 0:1]
    for s in range(1, SLOTS):
        copy(dqs.at[0], dqr.at[s], dq_ss, dq_rs, s, sibling).wait_recv()
        grad = grad + dqr[s].astype(F32) * shares[:OWN_Q, s : s + 1]
    dq_out[...] = grad.astype(BF16)

    for p in range(1, PIECES):
        copy(dkvs.at[:, 0], dkvr.at[p], out_ss, out_rs, p, sibling).wait_recv()
    for d in range(HEADS):
        total = dkvr[d].astype(F32) + dkvr[HEADS + d].astype(F32)
        columns = pl.ds(pl.multiple_of(lax.rem(head + d, HEADS) * DH, DH), DH)
        dk_out[:, columns] = total[0].astype(BF16)
        dv_out[:, columns] = total[1].astype(BF16)

    for started in sent:
        started.wait_send()


def to_vectors(x):
    return x.reshape(OWN_ROWS, PER_GROUP, DH).transpose(1, 0, 2).reshape(OWN_Q, DH)


def shards(queries, grad_out, outputs, lse_self, prompt_keys, prompt_values, resp_len, prompt_end):
    vmem = pl.BlockSpec(memory_space=pltpu.VMEM)
    smem = pl.BlockSpec(memory_space=pltpu.SMEM)

    def dma(n):
        return [pltpu.SemaphoreType.DMA((n,)), pltpu.SemaphoreType.DMA((n,))]

    dq, dk, dv = pl.pallas_call(
        kernel,
        out_shape=(
            jax.ShapeDtypeStruct((OWN_Q, DH), BF16),
            jax.ShapeDtypeStruct((PIECE, HEADS * DH), BF16),
            jax.ShapeDtypeStruct((PIECE, HEADS * DH), BF16),
        ),
        in_specs=[vmem] * 6 + [smem] * 2,
        out_specs=(vmem, vmem, vmem),
        scratch_shapes=[
            pltpu.VMEM((SLOTS, OWN_Q, DH), BF16),
            pltpu.VMEM((SLOTS, OWN_Q + 16, DH), BF16),
            pltpu.VMEM((HEADS, 2, PIECE, DH), BF16),
            pltpu.VMEM((2, 2, PIECES, PIECE, DH), BF16),
            pltpu.VMEM((SLOTS, ZS, DH), F32),
            pltpu.VMEM((ZS, DH), F32),
            pltpu.VMEM((ZS, DH), F32),
            pltpu.VMEM((NT, DH), jnp.int32),
            pltpu.VMEM((DH, NT), BF16),
            pltpu.VMEM((NT, NQ), BF16),
            pltpu.VMEM((NT, NQ), BF16),
            pltpu.VMEM((NQ, DH), BF16),
            pltpu.VMEM((NQ, DH), BF16),
            pltpu.VMEM((SLOTS, OWN_Q, DH), BF16),
            pltpu.VMEM((SLOTS, OWN_Q, DH), BF16),
            pltpu.VMEM((SLOTS, DH), F32),
            pltpu.VMEM((2, PIECES, PIECE, DH), BF16),
            pltpu.VMEM((2, PIECES, PIECE, DH), BF16),
            pltpu.VMEM((2, PIECES, PIECE, DH), BF16),
            pltpu.VMEM((PIECES, 2, PIECE, DH), BF16),
        ]
        + dma(SLOTS) + dma(SLOTS) + dma(PIECES) + dma(2) + dma(SLOTS) + dma(SLOTS)
        + dma(2) + dma(PIECES),
        compiler_params=pltpu.CompilerParams(
            collective_id=0, has_side_effects=True, vmem_limit_bytes=40 << 20
        ),
    )(
        to_vectors(queries), to_vectors(grad_out), to_vectors(outputs), lse_self,
        prompt_keys, prompt_values, resp_len, prompt_end,
    )
    query_grad = (
        dq.reshape(PER_GROUP, OWN_ROWS, DH).transpose(1, 0, 2).reshape(OWN_ROWS, PER_GROUP * DH)
    )
    return query_grad, dk, dv


def solution(mesh):
    in_specs = (
        P("ctx", "head"),
        P("ctx", "head"),
        P("ctx", "head"),
        P("ctx", "head"),
        P(("ctx", "head"), None),
        P(("ctx", "head"), None),
        P(),
        P(),
    )
    out_specs = (P("ctx", "head"), P(("ctx", "head"), None), P(("ctx", "head"), None))
    return jax.shard_map(shards, mesh=mesh, in_specs=in_specs, out_specs=out_specs, check_vma=False)
```

```python
import functools

import jax
import jax.numpy as jnp
from jax import lax
from jax.experimental import pallas as pl
from jax.experimental.pallas import tpu as pltpu
from jax.sharding import PartitionSpec as P

MESH = pl.DeviceIdType.MESH
F32 = jnp.float32
BF16 = jnp.bfloat16

DH = 128
HEADS = 8
PER_GROUP = 16
OWN_ROWS = 4
RESP_LEN = 64
YS, ZS = 4, 8
OWN_Q = OWN_ROWS * PER_GROUP
SLOTS = 2 * ZS
CHUNK = 2 * OWN_Q
NQ = SLOTS * OWN_Q
PIECE = 32
PIECES = 16
NT = 2 * PIECES * PIECE
SCALE = DH**-0.5
MASKED = -1e30
FLOOR = -1e20
DEAD = 1e30

NT_DIMS = (((1,), (1,)), ((), ()))


def realigned(part, dy, dz):
    halves = []
    for group in range(2):
        rows = part[group * 4 : group * 4 + 4]
        left, right = rows[:, :OWN_Q], rows[:, OWN_Q:]
        if dz % 2:
            left, right = rolled(right, dz // 2 + 1), rolled(left, dz // 2)
        else:
            left, right = rolled(left, dz // 2), rolled(right, dz // 2)
        halves.append(jnp.concatenate([left, right], axis=1))
    if dy:
        halves.reverse()
    return jnp.concatenate(halves, axis=0)


def rolled(x, by):
    by = by % 4
    return jnp.concatenate([x[4 - by :], x[: 4 - by]], axis=0) if by else x


def write_out(dq_in, dk_in, dv_in, dq_out, dk_out, dv_out, sems):
    copies = [
        pltpu.make_async_copy(src, dst, sems.at[i])
        for i, (src, dst) in enumerate(((dk_in, dk_out), (dv_in, dv_out), (dq_in, dq_out)))
    ]
    for copy in copies:
        copy.start()
    for copy in copies:
        copy.wait()


def kernel(
    q_hbm, do_hbm, o_hbm, lse_hbm, k_hbm, v_hbm, len_hbm, end_hbm,
    dq_out, dk_out, dv_out,
    o_in, lse_in, k_in, v_in, len_in, end_in, in_sems,
    qbuf, dobuf, kvs, kvbuf, lsebuf, mrow, lrow, posbuf, kt, ebuf, dsbuf, wq, wdo,
    dqs, dqr, dqy_s, dqy_r, fbuf, sib_s, sib_r, dkvs, dkvr,
    q_ss, q_rs, do_ss, do_rs, kv_ss, kv_rs, fwd_ss, fwd_rs, st_ss, st_rs, dq_ss, dq_rs, dqy_ss, dqy_rs,
    sib_ss, sib_rs, out_ss, out_rs,
):
    ctx = lax.axis_index("ctx")
    head = lax.axis_index("head")
    core = lax.rem(ctx, 2)
    z = lax.rem(ctx // 2, ZS)
    y = ctx // (2 * ZS)

    def device(yy, zz, cc, hh):
        return {
            "ctx": (lax.rem(yy + YS, YS) * ZS + lax.rem(zz + ZS, ZS)) * 2 + cc,
            "head": lax.rem(hh + HEADS, HEADS),
        }

    low = head < 4
    row_slots = [(s // ZS * 2, s % ZS) for s in range(SLOTS)]

    def back_slot(dy, dz):
        return dy // 2 * ZS + (ZS - dz) % ZS

    def row_device(s):
        dy, dz = row_slots[s]
        return device(y + dy, z + dz, core, head)

    def source_head(d):
        return lax.rem(head + HEADS - d, HEADS)

    def piece_y(p):
        if p < HEADS:
            return y
        return y + jnp.where(source_head(p - HEADS) < 4, 1, -1)

    def piece_device(p):
        return device(piece_y(p), z, core, source_head(p % HEADS))

    def user_device(p):
        if p < HEADS:
            return device(y, z, core, head + p)
        return device(y + jnp.where(low, -1, 1), z, core, head + p - HEADS)

    sibling = device(y, z, 1 - core, head)
    across = row_device(ZS)

    arrivals = [
        pltpu.make_async_copy(src, dst, in_sems.at[i])
        for i, (src, dst) in enumerate((
            (q_hbm, qbuf.at[0]), (do_hbm, dobuf.at[0, pl.ds(0, OWN_Q)]), (k_hbm, k_in),
            (v_hbm, v_in), (o_hbm, o_in), (lse_hbm, lse_in), (len_hbm, len_in),
            (end_hbm, end_in),
        ))
    ]
    for arrival in arrivals:
        arrival.start()

    barrier = pltpu.get_barrier_semaphore()
    greeted = [row_device(s) for s in range(1, ZS + 1)]
    greeted += [user_device(p) for p in range(1, PIECES)]
    greeted += [
        device(y + jnp.where(low, 1, -1), z, core, jnp.where(low, 0, 4) + i) for i in range(4)
    ]
    greeted += [sibling]
    for target in greeted:
        pl.semaphore_signal(barrier, inc=1, device_id=target, device_id_type=MESH)

    for arrival in arrivals:
        arrival.wait()
    prod = dobuf[0, :OWN_Q].astype(F32) * o_in[...].astype(F32)
    dots = jnp.sum(prod.T, axis=0, keepdims=True)
    dots = jnp.concatenate([dots, jnp.zeros((1, DH - OWN_Q), F32)], axis=1)
    high = dots.astype(BF16).astype(F32)
    middle = (dots - high).astype(BF16).astype(F32)
    rest = dots - high - middle
    dobuf[0, OWN_Q:] = jnp.concatenate(
        [high, middle, rest, jnp.zeros((13, DH), F32)], axis=0
    ).astype(BF16)
    for g in range(HEADS):
        kvs[g, 0] = k_in[:, g * DH : (g + 1) * DH]
        kvs[g, 1] = v_in[:, g * DH : (g + 1) * DH]
    pl.semaphore_wait(barrier, len(greeted))

    def copy(src, dst, ss, rs, i, target):
        return pltpu.make_async_remote_copy(
            src_ref=src, dst_ref=dst, send_sem=ss.at[i], recv_sem=rs.at[i],
            device_id=target, device_id_type=MESH,
        )

    sent = []

    def send(src, dst, ss, rs, i, target):
        started = copy(src, dst, ss, rs, i, target)
        started.start()
        sent.append(started)

    def kv_copy(p):
        return (
            kvs.at[lax.rem(head + p % HEADS, HEADS)], kvbuf.at[0, :, p], kv_ss, kv_rs, p,
            user_device(p),
        )

    def send_along(buf, ss, rs, s):
        for dz in range(1, ZS):
            send(buf.at[s], buf.at[s + ZS - dz], ss, rs, s + ZS - dz, row_device(dz))

    send(qbuf.at[0], qbuf.at[ZS], q_ss, q_rs, ZS, across)
    send(dobuf.at[0], dobuf.at[ZS], do_ss, do_rs, ZS, across)
    for p in range(1, PIECES):
        send(*kv_copy(p))
    send_along(qbuf, q_ss, q_rs, 0)
    send_along(dobuf, do_ss, do_rs, 0)

    kvbuf[0, :, 0] = kvs[head]

    iota = lax.broadcasted_iota(jnp.int32, (PIECE, DH), 0)
    for part in range(2):
        part_core = core if part == 0 else 1 - core
        for p in range(PIECES):
            place = (lax.rem(piece_y(p) + YS, YS) * ZS + z) * 2 + part_core
            base = place * (HEADS * PIECE) + source_head(p % HEADS) * PIECE
            posbuf[pl.ds((part * PIECES + p) * PIECE, PIECE), :] = iota + base
    lane = lax.broadcasted_iota(jnp.int32, (1, DH), 1)
    limits = (end_in[y], end_in[lax.rem(y + 2, YS)])

    lane64 = lax.broadcasted_iota(jnp.int32, (OWN_ROWS, OWN_Q), 1)
    sub64 = lax.broadcasted_iota(jnp.int32, (OWN_ROWS, OWN_Q), 0)
    spread = jnp.zeros((OWN_ROWS, OWN_Q), F32)
    for h in range(PER_GROUP):
        spread = jnp.where(lane64 // OWN_ROWS == h, lse_in[:, h : h + 1], spread)
    own_lse = jnp.sum(
        jnp.where(lane64 % OWN_ROWS == sub64, spread, 0.0), axis=0, keepdims=True
    )
    own_lse = jnp.concatenate([own_lse, jnp.full((1, DH - OWN_Q), MASKED, F32)], axis=1)
    row_in_resp = z * (2 * OWN_ROWS) + core * OWN_ROWS + lane % OWN_ROWS
    dead = jnp.logical_and(lane < OWN_Q, row_in_resp >= len_in[y])

    copy(qbuf.at[0], qbuf.at[ZS], q_ss, q_rs, ZS, sibling).wait_recv()
    send_along(qbuf, q_ss, q_rs, ZS)
    copy(dobuf.at[0], dobuf.at[ZS], do_ss, do_rs, ZS, sibling).wait_recv()
    send_along(dobuf, do_ss, do_rs, ZS)

    for p in range(1, PIECES):
        copy(*kv_copy(p)).wait_recv()
    for i in range(2):
        send(kvbuf.at[0, i], kvbuf.at[1, i], fwd_ss, fwd_rs, i, sibling)
    for i in range(2):
        copy(kvbuf.at[0, i], kvbuf.at[1, i], fwd_ss, fwd_rs, i, sibling).wait_recv()
    keys = kvbuf[:, 0].reshape(NT, DH)
    kt[...] = keys.T

    def wait_pair(buf, ss, rs, c):
        @pl.when(lax.rem(c, ZS // 2) > 0)
        def _():
            copy(buf.at[0], buf.at[2 * c], ss, rs, 2 * c, sibling).wait_recv()

        copy(buf.at[0], buf.at[2 * c + 1], ss, rs, 2 * c + 1, sibling).wait_recv()

    def score_step(c, carry):
        wait_pair(qbuf, q_ss, q_rs, c)
        limit = jnp.where(c < ZS // 2, limits[0], limits[1])
        queries = qbuf[pl.ds(2 * c, 2)].reshape(CHUNK, DH)
        scores = lax.dot_general(
            kvbuf[:, 0].reshape(NT, DH), queries, NT_DIMS, preferred_element_type=F32
        ) * SCALE
        scores = jnp.where(posbuf[...] < limit, scores, MASKED)
        peak = jnp.maximum(jnp.max(scores, axis=0, keepdims=True), FLOOR)
        terms = jnp.exp(scores - peak)
        total = jnp.sum(terms, axis=0, keepdims=True)
        ebuf[:, pl.ds(pl.multiple_of(c * CHUNK, CHUNK), CHUNK)] = terms.astype(BF16)
        mrow[pl.ds(c, 1), :] = peak
        lrow[pl.ds(c, 1), :] = total
        return carry

    lax.fori_loop(0, SLOTS // 2, score_step, 0)

    peaks = mrow[...]
    totals = lrow[...]
    local_lse = jnp.where(totals > 0.0, peaks + jnp.log(jnp.maximum(totals, 1e-37)), MASKED)
    first = local_lse[0:1]
    higher = jnp.maximum(first, own_lse)
    joined = higher + jnp.log(jnp.exp(first - higher) + jnp.exp(own_lse - higher))
    joined = jnp.where(lane < OWN_Q, jnp.where(dead, DEAD, joined), first)
    lsebuf[0] = jnp.concatenate([joined, local_lse[1:]], axis=0)
    for s in range(1, SLOTS):
        t = back_slot(*row_slots[s])
        send(lsebuf.at[0], lsebuf.at[t], st_ss, st_rs, t, row_device(s))
    lrow[...] = jnp.where(totals > 0.0, SCALE / jnp.maximum(totals, 1e-37), 0.0)

    def dscore_step(c, carry):
        wait_pair(dobuf, do_ss, do_rs, c)
        pair = dobuf[pl.ds(2 * c, 2)]
        grads = pair[:, :OWN_Q].reshape(CHUNK, DH)
        parts = pair[:, OWN_Q:].astype(F32)
        dots_pair = parts[:, 0:1] + parts[:, 1:2] + parts[:, 2:3]
        dots_row = jnp.concatenate([dots_pair[0, :, :OWN_Q], dots_pair[1, :, :OWN_Q]], axis=1)
        dprob = lax.dot_general(
            kvbuf[:, 1].reshape(NT, DH), grads, NT_DIMS, preferred_element_type=F32
        )
        columns = pl.ds(pl.multiple_of(c * CHUNK, CHUNK), CHUNK)
        dscore = (ebuf[:, columns].astype(F32) * (dprob - dots_row)).astype(BF16)
        dsbuf[:, columns] = dscore
        dq_t = jnp.dot(kt[...], dscore, preferred_element_type=F32)
        dq_t = dq_t * lrow[pl.ds(c, 1), :]
        dqs[pl.ds(2 * c, 2)] = dq_t.T.astype(BF16).reshape(2, OWN_Q, DH)
        return carry

    lax.fori_loop(0, SLOTS // 2, dscore_step, 0)

    for s in (0, ZS):
        for dz in range(1, ZS):
            t = s + ZS - dz
            send(dqs.at[s + dz], dqr.at[t], dq_ss, dq_rs, t, row_device(dz))

    aligned = []
    for s in range(SLOTS):
        if s > 0:
            copy(lsebuf.at[0], lsebuf.at[s], st_ss, st_rs, s, sibling).wait_recv()
        part = lsebuf[s]
        dy, dz = row_slots[s]
        aligned.append(realigned(part, dy, dz))
    top = functools.reduce(jnp.maximum, aligned)
    total = functools.reduce(jnp.add, [jnp.exp(part - top) for part in aligned])
    full_lse = top + jnp.log(total)
    for dz in range(ZS):
        for s, row in ((0, 0), (ZS, ZS // 2)):
            mine = local_lse[row : row + 1] if dz == 0 else aligned[dz][row : row + 1]
            fbuf[s + dz : s + dz + 1, :] = jnp.exp(mine - full_lse[row : row + 1])
    weight = jnp.exp(peaks - full_lse).T
    for c in range(SLOTS // 2):
        rows = slice(c * CHUNK, (c + 1) * CHUNK)
        column = weight[:, c : c + 1]
        wq[rows] = (
            qbuf[2 * c : 2 * c + 2].reshape(CHUNK, DH).astype(F32) * (column * SCALE)
        ).astype(BF16)
        wdo[rows] = (
            dobuf[2 * c : 2 * c + 2, :OWN_Q].reshape(CHUNK, DH).astype(F32) * column
        ).astype(BF16)

    half = PIECES * PIECE
    block = 256
    for i, (probs, weighted) in enumerate(((dsbuf, wq), (ebuf, wdo))):
        for b in range(half // block):
            rows = slice(half + b * block, half + (b + 1) * block)
            part = jnp.dot(probs[rows], weighted[...], preferred_element_type=F32)
            per = block // PIECE
            sib_s[i, b * per : (b + 1) * per] = part.astype(BF16).reshape(per, PIECE, DH)
        send(sib_s.at[i], sib_r.at[i], sib_ss, sib_rs, i, sibling)
    for i, (probs, weighted) in enumerate(((dsbuf, wq), (ebuf, wdo))):
        copy(sib_s.at[i], sib_r.at[i], sib_ss, sib_rs, i, sibling).wait_recv()
        for b in range(half // block):
            rows = slice(b * block, (b + 1) * block)
            part = jnp.dot(probs[rows], weighted[...], preferred_element_type=F32)
            per = block // PIECE
            pieces = slice(b * per, (b + 1) * per)
            dkvs[i, pieces] = (
                part.reshape(per, PIECE, DH) + sib_r[i, pieces].astype(F32)
            ).astype(BF16)

    for p in range(1, PIECES):
        send(dkvs.at[:, p], dkvr.at[p], out_ss, out_rs, p, piece_device(p))
    dkvr[0] = dkvs[:, 0]

    shares = fbuf[...].T

    def summed(s):
        grad = dqs[s].astype(F32) * shares[:OWN_Q, s : s + 1]
        for t in range(s + 1, s + ZS):
            copy(dqs.at[0], dqr.at[t], dq_ss, dq_rs, t, sibling).wait_recv()
            grad = grad + dqr[t].astype(F32) * shares[:OWN_Q, t : t + 1]
        return grad

    dqy_s[...] = summed(ZS)
    send(dqy_s, dqy_r, dqy_ss, dqy_rs, 0, across)
    grad = summed(0)
    copy(dqy_s, dqy_r, dqy_ss, dqy_rs, 0, sibling).wait_recv()
    dq_out[...] = (grad + dqy_r[...]).astype(BF16)

    for p in range(1, PIECES):
        copy(dkvs.at[:, 0], dkvr.at[p], out_ss, out_rs, p, sibling).wait_recv()
    for d in range(HEADS):
        total = dkvr[d].astype(F32) + dkvr[HEADS + d].astype(F32)
        columns = pl.ds(pl.multiple_of(lax.rem(head + d, HEADS) * DH, DH), DH)
        dk_out[:, columns] = total[0].astype(BF16)
        dv_out[:, columns] = total[1].astype(BF16)

    for started in sent:
        started.wait_send()


def to_vectors(x):
    return x.reshape(OWN_ROWS, PER_GROUP, DH).transpose(1, 0, 2).reshape(OWN_Q, DH)


def shards(queries, grad_out, outputs, lse_self, prompt_keys, prompt_values, resp_len, prompt_end):
    vmem = pl.BlockSpec(memory_space=pltpu.VMEM)
    anywhere = pl.BlockSpec(memory_space=pltpu.HBM)

    def dma(n):
        return [pltpu.SemaphoreType.DMA((n,)), pltpu.SemaphoreType.DMA((n,))]

    out_shape = (
        jax.ShapeDtypeStruct((OWN_Q, DH), BF16),
        jax.ShapeDtypeStruct((PIECE, HEADS * DH), BF16),
        jax.ShapeDtypeStruct((PIECE, HEADS * DH), BF16),
    )
    grads = pl.pallas_call(
        kernel,
        out_shape=out_shape,
        in_specs=[anywhere] * 8,
        out_specs=(vmem, vmem, vmem),
        scratch_shapes=[
            pltpu.VMEM((OWN_Q, DH), BF16),
            pltpu.VMEM((OWN_ROWS, PER_GROUP), F32),
            pltpu.VMEM((PIECE, HEADS * DH), BF16),
            pltpu.VMEM((PIECE, HEADS * DH), BF16),
            pltpu.SMEM((YS,), jnp.int32),
            pltpu.SMEM((YS,), jnp.int32),
            pltpu.SemaphoreType.DMA((8,)),
            pltpu.VMEM((SLOTS, OWN_Q, DH), BF16),
            pltpu.VMEM((SLOTS, OWN_Q + 16, DH), BF16),
            pltpu.VMEM((HEADS, 2, PIECE, DH), BF16),
            pltpu.VMEM((2, 2, PIECES, PIECE, DH), BF16),
            pltpu.VMEM((SLOTS, ZS, DH), F32),
            pltpu.VMEM((ZS, DH), F32),
            pltpu.VMEM((ZS, DH), F32),
            pltpu.VMEM((NT, DH), jnp.int32),
            pltpu.VMEM((DH, NT), BF16),
            pltpu.VMEM((NT, NQ), BF16),
            pltpu.VMEM((NT, NQ), BF16),
            pltpu.VMEM((NQ, DH), BF16),
            pltpu.VMEM((NQ, DH), BF16),
            pltpu.VMEM((SLOTS, OWN_Q, DH), BF16),
            pltpu.VMEM((SLOTS, OWN_Q, DH), BF16),
            pltpu.VMEM((OWN_Q, DH), F32),
            pltpu.VMEM((OWN_Q, DH), F32),
            pltpu.VMEM((SLOTS, DH), F32),
            pltpu.VMEM((2, PIECES, PIECE, DH), BF16),
            pltpu.VMEM((2, PIECES, PIECE, DH), BF16),
            pltpu.VMEM((2, PIECES, PIECE, DH), BF16),
            pltpu.VMEM((PIECES, 2, PIECE, DH), BF16),
        ]
        + dma(SLOTS) + dma(SLOTS) + dma(PIECES) + dma(2) + dma(SLOTS) + dma(SLOTS)
        + dma(1) + dma(2) + dma(PIECES),
        compiler_params=pltpu.CompilerParams(
            collective_id=0, has_side_effects=True, vmem_limit_bytes=64 << 20
        ),
    )(
        to_vectors(queries), to_vectors(grad_out), to_vectors(outputs), lse_self,
        prompt_keys, prompt_values, resp_len, prompt_end,
    )
    dq, dk, dv = pl.pallas_call(
        write_out,
        out_shape=out_shape,
        in_specs=[vmem] * 3,
        out_specs=(anywhere, anywhere, anywhere),
        scratch_shapes=[pltpu.SemaphoreType.DMA((3,))],
        compiler_params=pltpu.CompilerParams(vmem_limit_bytes=64 << 20),
    )(*grads)
    query_grad = (
        dq.reshape(PER_GROUP, OWN_ROWS, DH).transpose(1, 0, 2).reshape(OWN_ROWS, PER_GROUP * DH)
    )
    return query_grad, dk, dv


def solution(mesh):
    in_specs = (
        P("ctx", "head"),
        P("ctx", "head"),
        P("ctx", "head"),
        P("ctx", "head"),
        P(("ctx", "head"), None),
        P(("ctx", "head"), None),
        P(),
        P(),
    )
    out_specs = (P("ctx", "head"), P(("ctx", "head"), None), P(("ctx", "head"), None))
    return jax.shard_map(shards, mesh=mesh, in_specs=in_specs, out_specs=out_specs, check_vma=False)
```

```python
import functools

import jax
import jax.numpy as jnp
from jax import lax
from jax.experimental import pallas as pl
from jax.experimental.pallas import tpu as pltpu
from jax.sharding import PartitionSpec as P

MESH = pl.DeviceIdType.MESH
F32 = jnp.float32
BF16 = jnp.bfloat16

DH = 128
HEADS = 8
PER_GROUP = 16
OWN_ROWS = 4
RESP_LEN = 64
YS, ZS = 4, 8
OWN_Q = OWN_ROWS * PER_GROUP
SLOTS = 2 * ZS
PER_CHUNK = 4
CHUNK = PER_CHUNK * OWN_Q
ROW = 2 * OWN_Q
NQ = SLOTS * OWN_Q
PIECE = 32
PIECES = 16
NT = 2 * PIECES * PIECE
SCALE = DH**-0.5
MASKED = -1e30
FLOOR = -1e20
DEAD = 1e30

NT_DIMS = (((1,), (1,)), ((), ()))


def realigned(part, dy, dz):
    halves = []
    for group in range(2):
        rows = part[group * 4 : group * 4 + 4]
        left, right = rows[:, :OWN_Q], rows[:, OWN_Q:]
        if dz % 2:
            left, right = rolled(right, dz // 2 + 1), rolled(left, dz // 2)
        else:
            left, right = rolled(left, dz // 2), rolled(right, dz // 2)
        halves.append(jnp.concatenate([left, right], axis=1))
    if dy:
        halves.reverse()
    return jnp.concatenate(halves, axis=0)


def rolled(x, by):
    by = by % 4
    return jnp.concatenate([x[4 - by :], x[: 4 - by]], axis=0) if by else x


def write_out(dq_in, dk_in, dv_in, dq_out, dk_out, dv_out, sems):
    copies = [
        pltpu.make_async_copy(src, dst, sems.at[i])
        for i, (src, dst) in enumerate(((dk_in, dk_out), (dv_in, dv_out), (dq_in, dq_out)))
    ]
    for copy in copies:
        copy.start()
    for copy in copies:
        copy.wait()


def kernel(
    q_hbm, do_hbm, o_hbm, lse_hbm, k_hbm, v_hbm, len_hbm, end_hbm,
    dq_out, dk_out, dv_out,
    o_in, lse_in, k_in, v_in, len_in, end_in, in_sems,
    qbuf, dobuf, kvs, kvbuf, lsebuf, mrow, lrow, posbuf, kt, ebuf, dsbuf, wq, wdo,
    dqs, dqr, dqy_s, dqy_r, fbuf, sib_s, sib_r, dkvs, dkvr,
    q_ss, q_rs, do_ss, do_rs, kv_ss, kv_rs, fwd_ss, fwd_rs, st_ss, st_rs, dq_ss, dq_rs, dqy_ss, dqy_rs,
    sib_ss, sib_rs, out_ss, out_rs,
):
    ctx = lax.axis_index("ctx")
    head = lax.axis_index("head")
    core = lax.rem(ctx, 2)
    z = lax.rem(ctx // 2, ZS)
    y = ctx // (2 * ZS)

    def device(yy, zz, cc, hh):
        return {
            "ctx": (lax.rem(yy + YS, YS) * ZS + lax.rem(zz + ZS, ZS)) * 2 + cc,
            "head": lax.rem(hh + HEADS, HEADS),
        }

    low = head < 4
    row_slots = [(s // ZS * 2, s % ZS) for s in range(SLOTS)]

    def back_slot(dy, dz):
        return dy // 2 * ZS + (ZS - dz) % ZS

    def row_device(s):
        dy, dz = row_slots[s]
        return device(y + dy, z + dz, core, head)

    def source_head(d):
        return lax.rem(head + HEADS - d, HEADS)

    def piece_y(p):
        if p < HEADS:
            return y
        return y + jnp.where(source_head(p - HEADS) < 4, 1, -1)

    def piece_device(p):
        return device(piece_y(p), z, core, source_head(p % HEADS))

    def user_device(p):
        if p < HEADS:
            return device(y, z, core, head + p)
        return device(y + jnp.where(low, -1, 1), z, core, head + p - HEADS)

    sibling = device(y, z, 1 - core, head)
    across = row_device(ZS)

    arrivals = [
        pltpu.make_async_copy(src, dst, in_sems.at[i])
        for i, (src, dst) in enumerate((
            (q_hbm, qbuf.at[0]), (do_hbm, dobuf.at[0, pl.ds(0, OWN_Q)]), (k_hbm, k_in),
            (v_hbm, v_in), (o_hbm, o_in), (lse_hbm, lse_in), (len_hbm, len_in),
            (end_hbm, end_in),
        ))
    ]
    for arrival in arrivals:
        arrival.start()

    barrier = pltpu.get_barrier_semaphore()
    greeted = [row_device(s) for s in range(1, ZS + 1)]
    greeted += [user_device(p) for p in range(1, PIECES)]
    greeted += [
        device(y + jnp.where(low, 1, -1), z, core, jnp.where(low, 0, 4) + i) for i in range(4)
    ]
    greeted += [sibling]
    for target in greeted:
        pl.semaphore_signal(barrier, inc=1, device_id=target, device_id_type=MESH)

    for arrival in arrivals:
        arrival.wait()
    prod = dobuf[0, :OWN_Q].astype(F32) * o_in[...].astype(F32)
    dots = jnp.sum(prod.T, axis=0, keepdims=True)
    dots = jnp.concatenate([dots, jnp.zeros((1, DH - OWN_Q), F32)], axis=1)
    high = dots.astype(BF16).astype(F32)
    middle = (dots - high).astype(BF16).astype(F32)
    rest = dots - high - middle
    dobuf[0, OWN_Q:] = jnp.concatenate(
        [high, middle, rest, jnp.zeros((13, DH), F32)], axis=0
    ).astype(BF16)
    for g in range(HEADS):
        kvs[g, 0] = k_in[:, g * DH : (g + 1) * DH]
        kvs[g, 1] = v_in[:, g * DH : (g + 1) * DH]
    pl.semaphore_wait(barrier, len(greeted))

    def copy(src, dst, ss, rs, i, target):
        return pltpu.make_async_remote_copy(
            src_ref=src, dst_ref=dst, send_sem=ss.at[i], recv_sem=rs.at[i],
            device_id=target, device_id_type=MESH,
        )

    sent = []

    def send(src, dst, ss, rs, i, target):
        started = copy(src, dst, ss, rs, i, target)
        started.start()
        sent.append(started)

    def kv_copy(p):
        return (
            kvs.at[lax.rem(head + p % HEADS, HEADS)], kvbuf.at[0, :, p], kv_ss, kv_rs, p,
            user_device(p),
        )

    def send_along(buf, ss, rs, s):
        for dz in range(1, ZS):
            send(buf.at[s], buf.at[s + ZS - dz], ss, rs, s + ZS - dz, row_device(dz))

    send(qbuf.at[0], qbuf.at[ZS], q_ss, q_rs, ZS, across)
    send(dobuf.at[0], dobuf.at[ZS], do_ss, do_rs, ZS, across)
    for p in range(1, PIECES):
        send(*kv_copy(p))
    send_along(qbuf, q_ss, q_rs, 0)
    send_along(dobuf, do_ss, do_rs, 0)

    kvbuf[0, :, 0] = kvs[head]

    iota = lax.broadcasted_iota(jnp.int32, (PIECE, DH), 0)
    for part in range(2):
        part_core = core if part == 0 else 1 - core
        for p in range(PIECES):
            place = (lax.rem(piece_y(p) + YS, YS) * ZS + z) * 2 + part_core
            base = place * (HEADS * PIECE) + source_head(p % HEADS) * PIECE
            posbuf[pl.ds((part * PIECES + p) * PIECE, PIECE), :] = iota + base
    lane = lax.broadcasted_iota(jnp.int32, (1, DH), 1)
    limits = (end_in[y], end_in[lax.rem(y + 2, YS)])

    lane64 = lax.broadcasted_iota(jnp.int32, (OWN_ROWS, OWN_Q), 1)
    sub64 = lax.broadcasted_iota(jnp.int32, (OWN_ROWS, OWN_Q), 0)
    spread = jnp.zeros((OWN_ROWS, OWN_Q), F32)
    for h in range(PER_GROUP):
        spread = jnp.where(lane64 // OWN_ROWS == h, lse_in[:, h : h + 1], spread)
    own_lse = jnp.sum(
        jnp.where(lane64 % OWN_ROWS == sub64, spread, 0.0), axis=0, keepdims=True
    )
    own_lse = jnp.concatenate([own_lse, jnp.full((1, DH - OWN_Q), MASKED, F32)], axis=1)
    row_in_resp = z * (2 * OWN_ROWS) + core * OWN_ROWS + lane % OWN_ROWS
    dead = jnp.logical_and(lane < OWN_Q, row_in_resp >= len_in[y])

    copy(qbuf.at[0], qbuf.at[ZS], q_ss, q_rs, ZS, sibling).wait_recv()
    send_along(qbuf, q_ss, q_rs, ZS)
    copy(dobuf.at[0], dobuf.at[ZS], do_ss, do_rs, ZS, sibling).wait_recv()
    send_along(dobuf, do_ss, do_rs, ZS)

    for p in range(1, PIECES):
        copy(*kv_copy(p)).wait_recv()
    for i in range(2):
        send(kvbuf.at[0, i], kvbuf.at[1, i], fwd_ss, fwd_rs, i, sibling)
    for i in range(2):
        copy(kvbuf.at[0, i], kvbuf.at[1, i], fwd_ss, fwd_rs, i, sibling).wait_recv()
    keys = kvbuf[:, 0].reshape(NT, DH)
    kt[...] = keys.T

    def wait_chunk(buf, ss, rs, c):
        def wait(slot):
            copy(buf.at[0], buf.at[slot], ss, rs, slot, sibling).wait_recv()

        @pl.when(lax.rem(c, ZS // PER_CHUNK) > 0)
        def _():
            wait(PER_CHUNK * c)

        for i in range(1, PER_CHUNK):
            wait(PER_CHUNK * c + i)

    def score_step(c, carry):
        wait_chunk(qbuf, q_ss, q_rs, c)
        limit = jnp.where(c < ZS // PER_CHUNK, limits[0], limits[1])
        queries = qbuf[pl.ds(PER_CHUNK * c, PER_CHUNK)].reshape(CHUNK, DH)
        scores = lax.dot_general(
            kvbuf[:, 0].reshape(NT, DH), queries, NT_DIMS, preferred_element_type=F32
        ) * SCALE
        seen = posbuf[...] < limit
        scores = jnp.where(jnp.concatenate([seen] * (CHUNK // DH), axis=1), scores, MASKED)
        peak = jnp.maximum(jnp.max(scores, axis=0, keepdims=True), FLOOR)
        terms = jnp.exp(scores - peak)
        total = jnp.sum(terms, axis=0, keepdims=True)
        ebuf[:, pl.ds(pl.multiple_of(c * CHUNK, CHUNK), CHUNK)] = terms.astype(BF16)
        for i in range(CHUNK // ROW):
            row = pl.ds(CHUNK // ROW * c + i, 1)
            mrow[row, :] = peak[:, i * ROW : (i + 1) * ROW]
            lrow[row, :] = total[:, i * ROW : (i + 1) * ROW]
        return carry

    lax.fori_loop(0, SLOTS // PER_CHUNK, score_step, 0)

    peaks = mrow[...]
    totals = lrow[...]
    local_lse = jnp.where(totals > 0.0, peaks + jnp.log(jnp.maximum(totals, 1e-37)), MASKED)
    first = local_lse[0:1]
    higher = jnp.maximum(first, own_lse)
    joined = higher + jnp.log(jnp.exp(first - higher) + jnp.exp(own_lse - higher))
    joined = jnp.where(lane < OWN_Q, jnp.where(dead, DEAD, joined), first)
    lsebuf[0] = jnp.concatenate([joined, local_lse[1:]], axis=0)
    for s in range(1, SLOTS):
        t = back_slot(*row_slots[s])
        send(lsebuf.at[0], lsebuf.at[t], st_ss, st_rs, t, row_device(s))
    lrow[...] = jnp.where(totals > 0.0, SCALE / jnp.maximum(totals, 1e-37), 0.0)

    def dscore_step(c, carry):
        wait_chunk(dobuf, do_ss, do_rs, c)
        pair = dobuf[pl.ds(PER_CHUNK * c, PER_CHUNK)]
        grads = pair[:, :OWN_Q].reshape(CHUNK, DH)
        parts = pair[:, OWN_Q:].astype(F32)
        dots_pair = parts[:, 0:1] + parts[:, 1:2] + parts[:, 2:3]
        dots_row = jnp.concatenate([dots_pair[i, :, :OWN_Q] for i in range(PER_CHUNK)], axis=1)
        dprob = lax.dot_general(
            kvbuf[:, 1].reshape(NT, DH), grads, NT_DIMS, preferred_element_type=F32
        )
        columns = pl.ds(pl.multiple_of(c * CHUNK, CHUNK), CHUNK)
        dscore = (ebuf[:, columns].astype(F32) * (dprob - dots_row)).astype(BF16)
        dsbuf[:, columns] = dscore
        dq_t = jnp.dot(kt[...], dscore, preferred_element_type=F32)
        shares = [lrow[pl.ds(CHUNK // ROW * c + i, 1), :] for i in range(CHUNK // ROW)]
        dq_t = dq_t * jnp.concatenate(shares, axis=1)
        dqs[pl.ds(PER_CHUNK * c, PER_CHUNK)] = dq_t.T.astype(BF16).reshape(PER_CHUNK, OWN_Q, DH)
        return carry

    lax.fori_loop(0, SLOTS // PER_CHUNK, dscore_step, 0)

    for s in (0, ZS):
        for dz in range(1, ZS):
            t = s + ZS - dz
            send(dqs.at[s + dz], dqr.at[t], dq_ss, dq_rs, t, row_device(dz))

    aligned = []
    for s in range(SLOTS):
        if s > 0:
            copy(lsebuf.at[0], lsebuf.at[s], st_ss, st_rs, s, sibling).wait_recv()
        part = lsebuf[s]
        dy, dz = row_slots[s]
        aligned.append(realigned(part, dy, dz))
    top = functools.reduce(jnp.maximum, aligned)
    total = functools.reduce(jnp.add, [jnp.exp(part - top) for part in aligned])
    full_lse = top + jnp.log(total)
    for dz in range(ZS):
        for s, row in ((0, 0), (ZS, ZS // 2)):
            mine = local_lse[row : row + 1] if dz == 0 else aligned[dz][row : row + 1]
            fbuf[s + dz : s + dz + 1, :] = jnp.exp(mine - full_lse[row : row + 1])
    weight = jnp.exp(peaks - full_lse).T
    for c in range(SLOTS // 2):
        rows = slice(c * ROW, (c + 1) * ROW)
        column = weight[:, c : c + 1]
        wq[rows] = (
            qbuf[2 * c : 2 * c + 2].reshape(ROW, DH).astype(F32) * (column * SCALE)
        ).astype(BF16)
        wdo[rows] = (
            dobuf[2 * c : 2 * c + 2, :OWN_Q].reshape(ROW, DH).astype(F32) * column
        ).astype(BF16)

    half = PIECES * PIECE
    block = 256
    for i, (probs, weighted) in enumerate(((dsbuf, wq), (ebuf, wdo))):
        for b in range(half // block):
            rows = slice(half + b * block, half + (b + 1) * block)
            part = jnp.dot(probs[rows], weighted[...], preferred_element_type=F32)
            per = block // PIECE
            sib_s[i, b * per : (b + 1) * per] = part.astype(BF16).reshape(per, PIECE, DH)
        send(sib_s.at[i], sib_r.at[i], sib_ss, sib_rs, i, sibling)
    for i, (probs, weighted) in enumerate(((dsbuf, wq), (ebuf, wdo))):
        copy(sib_s.at[i], sib_r.at[i], sib_ss, sib_rs, i, sibling).wait_recv()
        for b in range(half // block):
            rows = slice(b * block, (b + 1) * block)
            part = jnp.dot(probs[rows], weighted[...], preferred_element_type=F32)
            per = block // PIECE
            pieces = slice(b * per, (b + 1) * per)
            dkvs[i, pieces] = (
                part.reshape(per, PIECE, DH) + sib_r[i, pieces].astype(F32)
            ).astype(BF16)
        for p in range(1, PIECES):
            send(
                dkvs.at[i, p], dkvr.at[p, i], out_ss, out_rs, i * PIECES + p, piece_device(p)
            )
        dkvr[0, i] = dkvs[i, 0]

    shares = fbuf[...].T

    def summed(s):
        grad = dqs[s].astype(F32) * shares[:OWN_Q, s : s + 1]
        for t in range(s + 1, s + ZS):
            copy(dqs.at[0], dqr.at[t], dq_ss, dq_rs, t, sibling).wait_recv()
            grad = grad + dqr[t].astype(F32) * shares[:OWN_Q, t : t + 1]
        return grad

    dqy_s[...] = summed(ZS)
    send(dqy_s, dqy_r, dqy_ss, dqy_rs, 0, across)
    grad = summed(0)
    copy(dqy_s, dqy_r, dqy_ss, dqy_rs, 0, sibling).wait_recv()
    dq_out[...] = (grad + dqy_r[...]).astype(BF16)

    for i in range(2):
        for p in range(1, PIECES):
            copy(
                dkvs.at[i, 0], dkvr.at[p, i], out_ss, out_rs, i * PIECES + p, sibling
            ).wait_recv()
    for d in range(HEADS):
        total = dkvr[d].astype(F32) + dkvr[HEADS + d].astype(F32)
        columns = pl.ds(pl.multiple_of(lax.rem(head + d, HEADS) * DH, DH), DH)
        dk_out[:, columns] = total[0].astype(BF16)
        dv_out[:, columns] = total[1].astype(BF16)

    for started in sent:
        started.wait_send()


def to_vectors(x):
    return x.reshape(OWN_ROWS, PER_GROUP, DH).transpose(1, 0, 2).reshape(OWN_Q, DH)


def shards(queries, grad_out, outputs, lse_self, prompt_keys, prompt_values, resp_len, prompt_end):
    vmem = pl.BlockSpec(memory_space=pltpu.VMEM)
    anywhere = pl.BlockSpec(memory_space=pltpu.HBM)

    def dma(n):
        return [pltpu.SemaphoreType.DMA((n,)), pltpu.SemaphoreType.DMA((n,))]

    out_shape = (
        jax.ShapeDtypeStruct((OWN_Q, DH), BF16),
        jax.ShapeDtypeStruct((PIECE, HEADS * DH), BF16),
        jax.ShapeDtypeStruct((PIECE, HEADS * DH), BF16),
    )
    grads = pl.pallas_call(
        kernel,
        out_shape=out_shape,
        in_specs=[anywhere] * 8,
        out_specs=(vmem, vmem, vmem),
        scratch_shapes=[
            pltpu.VMEM((OWN_Q, DH), BF16),
            pltpu.VMEM((OWN_ROWS, PER_GROUP), F32),
            pltpu.VMEM((PIECE, HEADS * DH), BF16),
            pltpu.VMEM((PIECE, HEADS * DH), BF16),
            pltpu.SMEM((YS,), jnp.int32),
            pltpu.SMEM((YS,), jnp.int32),
            pltpu.SemaphoreType.DMA((8,)),
            pltpu.VMEM((SLOTS, OWN_Q, DH), BF16),
            pltpu.VMEM((SLOTS, OWN_Q + 16, DH), BF16),
            pltpu.VMEM((HEADS, 2, PIECE, DH), BF16),
            pltpu.VMEM((2, 2, PIECES, PIECE, DH), BF16),
            pltpu.VMEM((SLOTS, ZS, DH), F32),
            pltpu.VMEM((ZS, DH), F32),
            pltpu.VMEM((ZS, DH), F32),
            pltpu.VMEM((NT, DH), jnp.int32),
            pltpu.VMEM((DH, NT), BF16),
            pltpu.VMEM((NT, NQ), BF16),
            pltpu.VMEM((NT, NQ), BF16),
            pltpu.VMEM((NQ, DH), BF16),
            pltpu.VMEM((NQ, DH), BF16),
            pltpu.VMEM((SLOTS, OWN_Q, DH), BF16),
            pltpu.VMEM((SLOTS, OWN_Q, DH), BF16),
            pltpu.VMEM((OWN_Q, DH), F32),
            pltpu.VMEM((OWN_Q, DH), F32),
            pltpu.VMEM((SLOTS, DH), F32),
            pltpu.VMEM((2, PIECES, PIECE, DH), BF16),
            pltpu.VMEM((2, PIECES, PIECE, DH), BF16),
            pltpu.VMEM((2, PIECES, PIECE, DH), BF16),
            pltpu.VMEM((PIECES, 2, PIECE, DH), BF16),
        ]
        + dma(SLOTS) + dma(SLOTS) + dma(PIECES) + dma(2) + dma(SLOTS) + dma(SLOTS)
        + dma(1) + dma(2) + dma(2 * PIECES),
        compiler_params=pltpu.CompilerParams(
            collective_id=0, has_side_effects=True, vmem_limit_bytes=64 << 20
        ),
    )(
        to_vectors(queries), to_vectors(grad_out), to_vectors(outputs), lse_self,
        prompt_keys, prompt_values, resp_len, prompt_end,
    )
    dq, dk, dv = pl.pallas_call(
        write_out,
        out_shape=out_shape,
        in_specs=[vmem] * 3,
        out_specs=(anywhere, anywhere, anywhere),
        scratch_shapes=[pltpu.SemaphoreType.DMA((3,))],
        compiler_params=pltpu.CompilerParams(vmem_limit_bytes=64 << 20),
    )(*grads)
    query_grad = (
        dq.reshape(PER_GROUP, OWN_ROWS, DH).transpose(1, 0, 2).reshape(OWN_ROWS, PER_GROUP * DH)
    )
    return query_grad, dk, dv


def solution(mesh):
    in_specs = (
        P("ctx", "head"),
        P("ctx", "head"),
        P("ctx", "head"),
        P("ctx", "head"),
        P(("ctx", "head"), None),
        P(("ctx", "head"), None),
        P(),
        P(),
    )
    out_specs = (P("ctx", "head"), P(("ctx", "head"), None), P(("ctx", "head"), None))
    return jax.shard_map(shards, mesh=mesh, in_specs=in_specs, out_specs=out_specs, check_vma=False)
```

```python
import functools

import jax
import jax.numpy as jnp
from jax import lax
from jax.experimental import pallas as pl
from jax.experimental.pallas import tpu as pltpu
from jax.sharding import PartitionSpec as P

MESH = pl.DeviceIdType.MESH
F32 = jnp.float32
BF16 = jnp.bfloat16

DH = 128
HEADS = 8
PER_GROUP = 16
OWN_ROWS = 4
RESP_LEN = 64
YS, ZS = 4, 8
OWN_Q = OWN_ROWS * PER_GROUP
SLOTS = 2 * ZS
PER_CHUNK = 4
CHUNK = PER_CHUNK * OWN_Q
ROW = 2 * OWN_Q
NQ = SLOTS * OWN_Q
PIECE = 32
PIECES = 16
NT = 2 * PIECES * PIECE
SCALE = DH**-0.5
MASKED = -1e30
FLOOR = -1e20
DEAD = 1e30

NT_DIMS = (((1,), (1,)), ((), ()))


def realigned(part, dy, dz):
    halves = []
    for group in range(2):
        rows = part[group * 4 : group * 4 + 4]
        left, right = rows[:, :OWN_Q], rows[:, OWN_Q:]
        if dz % 2:
            left, right = rolled(right, dz // 2 + 1), rolled(left, dz // 2)
        else:
            left, right = rolled(left, dz // 2), rolled(right, dz // 2)
        halves.append(jnp.concatenate([left, right], axis=1))
    if dy:
        halves.reverse()
    return jnp.concatenate(halves, axis=0)


def rolled(x, by):
    by = by % 4
    return jnp.concatenate([x[4 - by :], x[: 4 - by]], axis=0) if by else x


def write_out(dq_in, dk_in, dv_in, dq_out, dk_out, dv_out, sems):
    copies = [
        pltpu.make_async_copy(src, dst, sems.at[i])
        for i, (src, dst) in enumerate(((dk_in, dk_out), (dv_in, dv_out), (dq_in, dq_out)))
    ]
    for copy in copies:
        copy.start()
    for copy in copies:
        copy.wait()


def kernel(
    q_hbm, do_hbm, o_hbm, lse_hbm, k_hbm, v_hbm, len_hbm, end_hbm,
    dq_out, dk_out, dv_out,
    o_in, lse_in, k_in, v_in, len_in, end_in, in_sems,
    qbuf, dobuf, dotbuf, kvs, kvbuf, lsebuf, mrow, lrow, posbuf, kt, ebuf, dsbuf, wq, wdo,
    dqs, dqr, dqy_s, dqy_r, fbuf, sib_s, sib_r, dkvs, dkvr,
    q_ss, q_rs, do_ss, do_rs, dot_ss, dot_rs, kv_ss, kv_rs, fwd_ss, fwd_rs, st_ss, st_rs, dq_ss, dq_rs, dqy_ss, dqy_rs,
    sib_ss, sib_rs, out_ss, out_rs,
):
    ctx = lax.axis_index("ctx")
    head = lax.axis_index("head")
    core = lax.rem(ctx, 2)
    z = lax.rem(ctx // 2, ZS)
    y = ctx // (2 * ZS)

    def device(yy, zz, cc, hh):
        return {
            "ctx": (lax.rem(yy + YS, YS) * ZS + lax.rem(zz + ZS, ZS)) * 2 + cc,
            "head": lax.rem(hh + HEADS, HEADS),
        }

    low = head < 4
    row_slots = [(s // ZS * 2, s % ZS) for s in range(SLOTS)]

    def back_slot(dy, dz):
        return dy // 2 * ZS + (ZS - dz) % ZS

    def row_device(s):
        dy, dz = row_slots[s]
        return device(y + dy, z + dz, core, head)

    def source_head(d):
        return lax.rem(head + HEADS - d, HEADS)

    def piece_y(p):
        if p < HEADS:
            return y
        return y + jnp.where(source_head(p - HEADS) < 4, 1, -1)

    def piece_device(p):
        return device(piece_y(p), z, core, source_head(p % HEADS))

    def user_device(p):
        if p < HEADS:
            return device(y, z, core, head + p)
        return device(y + jnp.where(low, -1, 1), z, core, head + p - HEADS)

    sibling = device(y, z, 1 - core, head)
    across = row_device(ZS)

    arrivals = [
        pltpu.make_async_copy(src, dst, in_sems.at[i])
        for i, (src, dst) in enumerate((
            (q_hbm, qbuf.at[0]), (do_hbm, dobuf.at[0]), (k_hbm, k_in),
            (v_hbm, v_in), (o_hbm, o_in), (lse_hbm, lse_in), (len_hbm, len_in),
            (end_hbm, end_in),
        ))
    ]
    for arrival in arrivals:
        arrival.start()

    barrier = pltpu.get_barrier_semaphore()
    greeted = [row_device(s) for s in (ZS, 4, 3, 5, 2, 6, 1, 7)]
    greeted += [user_device(p) for p in range(1, PIECES)]
    greeted += [
        device(y + jnp.where(low, 1, -1), z, core, jnp.where(low, 0, 4) + i) for i in range(4)
    ]
    greeted += [sibling]
    for target in greeted:
        pl.semaphore_signal(barrier, inc=1, device_id=target, device_id_type=MESH)

    def copy(src, dst, ss, rs, i, target):
        return pltpu.make_async_remote_copy(
            src_ref=src, dst_ref=dst, send_sem=ss.at[i], recv_sem=rs.at[i],
            device_id=target, device_id_type=MESH,
        )

    sent = []

    def send(src, dst, ss, rs, i, target):
        started = copy(src, dst, ss, rs, i, target)
        started.start()
        sent.append(started)

    def kv_copy(p):
        return (
            kvs.at[lax.rem(head + p % HEADS, HEADS)], kvbuf.at[0, :, p], kv_ss, kv_rs, p,
            user_device(p),
        )

    def send_along(buf, ss, rs, s):
        for dz in range(1, ZS):
            send(buf.at[s], buf.at[s + ZS - dz], ss, rs, s + ZS - dz, row_device(dz))

    q_arrival, do_arrival, k_arrival, v_arrival, *others = arrivals
    q_arrival.wait()
    pl.semaphore_wait(barrier, len(greeted))
    send(qbuf.at[0], qbuf.at[ZS], q_ss, q_rs, ZS, across)
    send_along(qbuf, q_ss, q_rs, 0)
    k_arrival.wait()
    v_arrival.wait()
    for g in range(HEADS):
        kvs[g, 0] = k_in[:, g * DH : (g + 1) * DH]
        kvs[g, 1] = v_in[:, g * DH : (g + 1) * DH]
    for p in range(1, PIECES):
        send(*kv_copy(p))
    do_arrival.wait()
    for arrival in others:
        arrival.wait()
    prod = dobuf[0].astype(F32) * o_in[...].astype(F32)
    dots = jnp.sum(prod.T, axis=0, keepdims=True)
    dotbuf[0] = jnp.concatenate([dots, jnp.zeros((1, DH - OWN_Q), F32)], axis=1)
    send(dobuf.at[0], dobuf.at[ZS], do_ss, do_rs, ZS, across)
    send(dotbuf.at[0], dotbuf.at[ZS], dot_ss, dot_rs, ZS, across)
    send_along(dobuf, do_ss, do_rs, 0)
    send_along(dotbuf, dot_ss, dot_rs, 0)

    kvbuf[0, :, 0] = kvs[head]

    iota = lax.broadcasted_iota(jnp.int32, (PIECE, DH), 0)
    for part in range(2):
        part_core = core if part == 0 else 1 - core
        for p in range(PIECES):
            place = (lax.rem(piece_y(p) + YS, YS) * ZS + z) * 2 + part_core
            base = place * (HEADS * PIECE) + source_head(p % HEADS) * PIECE
            posbuf[pl.ds((part * PIECES + p) * PIECE, PIECE), :] = iota + base
    lane = lax.broadcasted_iota(jnp.int32, (1, DH), 1)
    limits = (end_in[y], end_in[lax.rem(y + 2, YS)])

    lane64 = lax.broadcasted_iota(jnp.int32, (OWN_ROWS, OWN_Q), 1)
    sub64 = lax.broadcasted_iota(jnp.int32, (OWN_ROWS, OWN_Q), 0)
    spread = jnp.zeros((OWN_ROWS, OWN_Q), F32)
    for h in range(PER_GROUP):
        spread = jnp.where(lane64 // OWN_ROWS == h, lse_in[:, h : h + 1], spread)
    own_lse = jnp.sum(
        jnp.where(lane64 % OWN_ROWS == sub64, spread, 0.0), axis=0, keepdims=True
    )
    own_lse = jnp.concatenate([own_lse, jnp.full((1, DH - OWN_Q), MASKED, F32)], axis=1)
    row_in_resp = z * (2 * OWN_ROWS) + core * OWN_ROWS + lane % OWN_ROWS
    dead = jnp.logical_and(lane < OWN_Q, row_in_resp >= len_in[y])

    copy(qbuf.at[0], qbuf.at[ZS], q_ss, q_rs, ZS, sibling).wait_recv()
    send_along(qbuf, q_ss, q_rs, ZS)
    copy(dobuf.at[0], dobuf.at[ZS], do_ss, do_rs, ZS, sibling).wait_recv()
    send_along(dobuf, do_ss, do_rs, ZS)
    copy(dotbuf.at[0], dotbuf.at[ZS], dot_ss, dot_rs, ZS, sibling).wait_recv()
    send_along(dotbuf, dot_ss, dot_rs, ZS)

    for p in range(1, PIECES):
        copy(*kv_copy(p)).wait_recv()
    for i in range(2):
        send(kvbuf.at[0, i], kvbuf.at[1, i], fwd_ss, fwd_rs, i, sibling)
    for i in range(2):
        copy(kvbuf.at[0, i], kvbuf.at[1, i], fwd_ss, fwd_rs, i, sibling).wait_recv()
    keys = kvbuf[:, 0].reshape(NT, DH)
    kt[...] = keys.T

    def wait_chunk(buf, ss, rs, c):
        def wait(slot):
            copy(buf.at[0], buf.at[slot], ss, rs, slot, sibling).wait_recv()

        @pl.when(lax.rem(c, ZS // PER_CHUNK) > 0)
        def _():
            wait(PER_CHUNK * c)

        for i in range(1, PER_CHUNK):
            wait(PER_CHUNK * c + i)

    def score_step(c, carry):
        wait_chunk(qbuf, q_ss, q_rs, c)
        limit = jnp.where(c < ZS // PER_CHUNK, limits[0], limits[1])
        queries = qbuf[pl.ds(PER_CHUNK * c, PER_CHUNK)].reshape(CHUNK, DH)
        scores = lax.dot_general(
            kvbuf[:, 0].reshape(NT, DH), queries, NT_DIMS, preferred_element_type=F32
        ) * SCALE
        seen = posbuf[...] < limit
        scores = jnp.where(jnp.concatenate([seen] * (CHUNK // DH), axis=1), scores, MASKED)
        peak = jnp.maximum(jnp.max(scores, axis=0, keepdims=True), FLOOR)
        terms = jnp.exp(scores - peak)
        total = jnp.sum(terms, axis=0, keepdims=True)
        ebuf[:, pl.ds(pl.multiple_of(c * CHUNK, CHUNK), CHUNK)] = terms.astype(BF16)
        for i in range(CHUNK // ROW):
            row = pl.ds(CHUNK // ROW * c + i, 1)
            mrow[row, :] = peak[:, i * ROW : (i + 1) * ROW]
            lrow[row, :] = total[:, i * ROW : (i + 1) * ROW]
        return carry

    lax.fori_loop(0, SLOTS // PER_CHUNK, score_step, 0)

    peaks = mrow[...]
    totals = lrow[...]
    local_lse = jnp.where(totals > 0.0, peaks + jnp.log(jnp.maximum(totals, 1e-37)), MASKED)
    first = local_lse[0:1]
    higher = jnp.maximum(first, own_lse)
    joined = higher + jnp.log(jnp.exp(first - higher) + jnp.exp(own_lse - higher))
    joined = jnp.where(lane < OWN_Q, jnp.where(dead, DEAD, joined), first)
    lsebuf[0] = jnp.concatenate([joined, local_lse[1:]], axis=0)
    for s in range(1, SLOTS):
        t = back_slot(*row_slots[s])
        send(lsebuf.at[0], lsebuf.at[t], st_ss, st_rs, t, row_device(s))
    lrow[...] = jnp.where(totals > 0.0, SCALE / jnp.maximum(totals, 1e-37), 0.0)

    def dscore_step(c, carry):
        wait_chunk(dobuf, do_ss, do_rs, c)
        wait_chunk(dotbuf, dot_ss, dot_rs, c)
        grads = dobuf[pl.ds(PER_CHUNK * c, PER_CHUNK)].reshape(CHUNK, DH)
        row = dotbuf[pl.ds(PER_CHUNK * c, PER_CHUNK)]
        dots_row = jnp.concatenate([row[i, :, :OWN_Q] for i in range(PER_CHUNK)], axis=1)
        dprob = lax.dot_general(
            kvbuf[:, 1].reshape(NT, DH), grads, NT_DIMS, preferred_element_type=F32
        )
        columns = pl.ds(pl.multiple_of(c * CHUNK, CHUNK), CHUNK)
        dscore = (ebuf[:, columns].astype(F32) * (dprob - dots_row)).astype(BF16)
        dsbuf[:, columns] = dscore
        dq_t = jnp.dot(kt[...], dscore, preferred_element_type=F32)
        shares = [lrow[pl.ds(CHUNK // ROW * c + i, 1), :] for i in range(CHUNK // ROW)]
        dq_t = dq_t * jnp.concatenate(shares, axis=1)
        dqs[pl.ds(PER_CHUNK * c, PER_CHUNK)] = dq_t.T.astype(BF16).reshape(PER_CHUNK, OWN_Q, DH)
        return carry

    lax.fori_loop(0, SLOTS // PER_CHUNK, dscore_step, 0)

    for s in (0, ZS):
        for dz in range(1, ZS):
            t = s + ZS - dz
            send(dqs.at[s + dz], dqr.at[t], dq_ss, dq_rs, t, row_device(dz))

    aligned = []
    for s in range(SLOTS):
        if s > 0:
            copy(lsebuf.at[0], lsebuf.at[s], st_ss, st_rs, s, sibling).wait_recv()
        part = lsebuf[s]
        dy, dz = row_slots[s]
        aligned.append(realigned(part, dy, dz))
    top = functools.reduce(jnp.maximum, aligned)
    total = functools.reduce(jnp.add, [jnp.exp(part - top) for part in aligned])
    full_lse = top + jnp.log(total)
    weight = jnp.exp(peaks - full_lse).T
    for c in range(SLOTS // 2):
        rows = slice(c * ROW, (c + 1) * ROW)
        column = weight[:, c : c + 1]
        wq[rows] = (
            qbuf[2 * c : 2 * c + 2].reshape(ROW, DH).astype(F32) * (column * SCALE)
        ).astype(BF16)
        wdo[rows] = (
            dobuf[2 * c : 2 * c + 2].reshape(ROW, DH).astype(F32) * column
        ).astype(BF16)

    half = PIECES * PIECE
    block = 256
    for i, (probs, weighted) in enumerate(((dsbuf, wq), (ebuf, wdo))):
        for b in range(half // block):
            rows = slice(half + b * block, half + (b + 1) * block)
            part = jnp.dot(probs[rows], weighted[...], preferred_element_type=F32)
            per = block // PIECE
            sib_s[i, b * per : (b + 1) * per] = part.astype(BF16).reshape(per, PIECE, DH)
        send(sib_s.at[i], sib_r.at[i], sib_ss, sib_rs, i, sibling)
    for i, (probs, weighted) in enumerate(((dsbuf, wq), (ebuf, wdo))):
        copy(sib_s.at[i], sib_r.at[i], sib_ss, sib_rs, i, sibling).wait_recv()
        for b in range(half // block):
            rows = slice(b * block, (b + 1) * block)
            part = jnp.dot(probs[rows], weighted[...], preferred_element_type=F32)
            per = block // PIECE
            pieces = slice(b * per, (b + 1) * per)
            dkvs[i, pieces] = (
                part.reshape(per, PIECE, DH) + sib_r[i, pieces].astype(F32)
            ).astype(BF16)
        for p in range(1, PIECES):
            send(
                dkvs.at[i, p], dkvr.at[p, i], out_ss, out_rs, i * PIECES + p, piece_device(p)
            )
        dkvr[0, i] = dkvs[i, 0]

    for dz in range(ZS):
        for s, row in ((0, 0), (ZS, ZS // 2)):
            mine = local_lse[row : row + 1] if dz == 0 else aligned[dz][row : row + 1]
            fbuf[s + dz : s + dz + 1, :] = jnp.exp(mine - full_lse[row : row + 1])
    shares = fbuf[...].T

    def summed(s):
        grad = dqs[s].astype(F32) * shares[:OWN_Q, s : s + 1]
        for t in range(s + 1, s + ZS):
            copy(dqs.at[0], dqr.at[t], dq_ss, dq_rs, t, sibling).wait_recv()
            grad = grad + dqr[t].astype(F32) * shares[:OWN_Q, t : t + 1]
        return grad

    dqy_s[...] = summed(ZS)
    send(dqy_s, dqy_r, dqy_ss, dqy_rs, 0, across)
    grad = summed(0)
    copy(dqy_s, dqy_r, dqy_ss, dqy_rs, 0, sibling).wait_recv()
    dq_out[...] = (grad + dqy_r[...]).astype(BF16)

    for i in range(2):
        for p in range(1, PIECES):
            copy(
                dkvs.at[i, 0], dkvr.at[p, i], out_ss, out_rs, i * PIECES + p, sibling
            ).wait_recv()
    for d in range(HEADS):
        total = dkvr[d].astype(F32) + dkvr[HEADS + d].astype(F32)
        columns = pl.ds(pl.multiple_of(lax.rem(head + d, HEADS) * DH, DH), DH)
        dk_out[:, columns] = total[0].astype(BF16)
        dv_out[:, columns] = total[1].astype(BF16)

    for started in sent:
        started.wait_send()


def to_vectors(x):
    return x.reshape(OWN_ROWS, PER_GROUP, DH).transpose(1, 0, 2).reshape(OWN_Q, DH)


def shards(queries, grad_out, outputs, lse_self, prompt_keys, prompt_values, resp_len, prompt_end):
    vmem = pl.BlockSpec(memory_space=pltpu.VMEM)
    anywhere = pl.BlockSpec(memory_space=pltpu.HBM)

    def dma(n):
        return [pltpu.SemaphoreType.DMA((n,)), pltpu.SemaphoreType.DMA((n,))]

    out_shape = (
        jax.ShapeDtypeStruct((OWN_Q, DH), BF16),
        jax.ShapeDtypeStruct((PIECE, HEADS * DH), BF16),
        jax.ShapeDtypeStruct((PIECE, HEADS * DH), BF16),
    )
    grads = pl.pallas_call(
        kernel,
        out_shape=out_shape,
        in_specs=[anywhere] * 8,
        out_specs=(vmem, vmem, vmem),
        scratch_shapes=[
            pltpu.VMEM((OWN_Q, DH), BF16),
            pltpu.VMEM((OWN_ROWS, PER_GROUP), F32),
            pltpu.VMEM((PIECE, HEADS * DH), BF16),
            pltpu.VMEM((PIECE, HEADS * DH), BF16),
            pltpu.SMEM((YS,), jnp.int32),
            pltpu.SMEM((YS,), jnp.int32),
            pltpu.SemaphoreType.DMA((8,)),
            pltpu.VMEM((SLOTS, OWN_Q, DH), BF16),
            pltpu.VMEM((SLOTS, OWN_Q, DH), BF16),
            pltpu.VMEM((SLOTS, 1, DH), F32),
            pltpu.VMEM((HEADS, 2, PIECE, DH), BF16),
            pltpu.VMEM((2, 2, PIECES, PIECE, DH), BF16),
            pltpu.VMEM((SLOTS, ZS, DH), F32),
            pltpu.VMEM((ZS, DH), F32),
            pltpu.VMEM((ZS, DH), F32),
            pltpu.VMEM((NT, DH), jnp.int32),
            pltpu.VMEM((DH, NT), BF16),
            pltpu.VMEM((NT, NQ), BF16),
            pltpu.VMEM((NT, NQ), BF16),
            pltpu.VMEM((NQ, DH), BF16),
            pltpu.VMEM((NQ, DH), BF16),
            pltpu.VMEM((SLOTS, OWN_Q, DH), BF16),
            pltpu.VMEM((SLOTS, OWN_Q, DH), BF16),
            pltpu.VMEM((OWN_Q, DH), F32),
            pltpu.VMEM((OWN_Q, DH), F32),
            pltpu.VMEM((SLOTS, DH), F32),
            pltpu.VMEM((2, PIECES, PIECE, DH), BF16),
            pltpu.VMEM((2, PIECES, PIECE, DH), BF16),
            pltpu.VMEM((2, PIECES, PIECE, DH), BF16),
            pltpu.VMEM((PIECES, 2, PIECE, DH), BF16),
        ]
        + dma(SLOTS) + dma(SLOTS) + dma(SLOTS) + dma(PIECES) + dma(2) + dma(SLOTS) + dma(SLOTS)
        + dma(1) + dma(2) + dma(2 * PIECES),
        compiler_params=pltpu.CompilerParams(
            collective_id=0, has_side_effects=True, vmem_limit_bytes=64 << 20
        ),
    )(
        to_vectors(queries), to_vectors(grad_out), to_vectors(outputs), lse_self,
        prompt_keys, prompt_values, resp_len, prompt_end,
    )
    dq, dk, dv = pl.pallas_call(
        write_out,
        out_shape=out_shape,
        in_specs=[vmem] * 3,
        out_specs=(anywhere, anywhere, anywhere),
        scratch_shapes=[pltpu.SemaphoreType.DMA((3,))],
        compiler_params=pltpu.CompilerParams(vmem_limit_bytes=64 << 20),
    )(*grads)
    query_grad = (
        dq.reshape(PER_GROUP, OWN_ROWS, DH).transpose(1, 0, 2).reshape(OWN_ROWS, PER_GROUP * DH)
    )
    return query_grad, dk, dv


def solution(mesh):
    in_specs = (
        P("ctx", "head"),
        P("ctx", "head"),
        P("ctx", "head"),
        P("ctx", "head"),
        P(("ctx", "head"), None),
        P(("ctx", "head"), None),
        P(),
        P(),
    )
    out_specs = (P("ctx", "head"), P(("ctx", "head"), None), P(("ctx", "head"), None))
    return jax.shard_map(shards, mesh=mesh, in_specs=in_specs, out_specs=out_specs, check_vma=False)
```
